32 devices in a mesh: panel: 2 (over core), colat: 4 (over z), lon: 4 (over y, x).
Axes of the slice: x: 2, y: 2, z: 4, core: 2. Of those that a mesh axis runs over, the one named last changes fastest.
Arguments:
- state: float32 [2, 4, 8, 128, 512], P('panel', None, None, 'lon', 'colat'), may hold values from -6 to 6
- rhs: float32 [2, 4, 8, 128, 512], P('panel', None, None, 'lon', 'colat'), may hold values from -6 to 6
- viscosity: float32 [2, 8, 128, 512], P('panel', None, 'lon', 'colat'), may hold values from 0.25 to 4
- radial_bounds: int32 [2, 2], P('panel'), may hold values from 0 to 8, as said below
- partner_device: int32 [2, 4, 4, 8], P('panel', 'colat', 'lon'), may hold values from 0 to 15, as said below
- ghost_source: int32 [2, 4, 4, 8, 20], P('panel', 'colat', 'lon'), may hold values from 0 to 3966, as said below
- ghost_target: int32 [2, 4, 4, 8, 20], P('panel', 'colat', 'lon'), may hold values from 0 to 320, as said below
- interp_weights: float32 [2, 4, 4, 8, 4, 20], P('panel', 'colat', 'lon'), may hold values from 0 to 1, as said below
- rotation: float32 [2, 4, 4, 8, 20], P('panel', 'colat', 'lon'), may hold values from -3.140625 to 3.140625
Outputs:
- state_out: float32 [2, 4, 8, 128, 512], P('panel', None, None, 'lon', 'colat')
- residual: float32 [2, 4, 8, 128, 512], P('panel', None, None, 'lon', 'colat')
The draws below stay inside these ranges and needn't reach their ends.
Inputs may be any that keep to these rules, and one draw needn't show every extreme that they name: For each panel a, radial_bounds[a, 0] < 4 and radial_bounds[a, 1] > 4. `partner_device`: A device's 8 partners are distinct devices of the other panel, numbered colatitude block times 4 plus longitude block; they are consecutive numbers counted round and include the number one below the device's own number. `ghost_source`: A value p * 128 + t with t < 127 and p < 31, local to the partner's block. `ghost_target`: each ghost cell of a device that lies beyond an edge of the panel is named by exactly one of that device's slots and no other ghost cell by any; used slots come first in the order partner, slot, and unused ones hold 320. `interp_weights`: the four weights of a slot are nonnegative and sum to one.
All inputs are finite; a program needn't handle non-finite values.
Results may differ from the reference program's by a relative error of at most 0.0003.
Values sent between devices are 32-bit elements; how exact they have to be, the bound alone decides.
A program may use at most 128 MiB of HBM per device.

```python
import math
import jax
import jax.numpy as jnp

NR = 8
CT = 128
CP = 32
PARTNERS = 8
SLOTS = 20
GHOSTS = 320
COLAT_BLOCKS = 4
LON_BLOCKS = 4
PANEL_DEVICES = 16
NT = 512
NP = 128


def draw_radial_bounds(key, part):
    key = jax.random.fold_in(key, 11)
    key_lower, key_upper = jax.random.split(key)
    lower = jax.random.randint(key_lower, (2, 1), 0, NR // 2)
    upper = jax.random.randint(key_upper, (2, 1), NR // 2 + 1, NR + 1)
    return jnp.concatenate([lower, upper], axis=-1).astype(jnp.int32)


def draw_partner_device(key, part):
    key = jax.random.fold_in(key, 12)
    own_number = (jnp.arange(COLAT_BLOCKS)[:, None] * LON_BLOCKS + jnp.arange(LON_BLOCKS)[None, :])[None, :, :, None]
    offset = jax.random.randint(key, (2, COLAT_BLOCKS, LON_BLOCKS, 1), 0, PARTNERS - 1)
    base_device = own_number - 1 - offset + PANEL_DEVICES
    return ((base_device + jnp.arange(PARTNERS)[None, None, None, :]) % PANEL_DEVICES).astype(jnp.int32)


def draw_ghost_source(key, part):
    key = jax.random.fold_in(key, 13)
    key_colat, key_lon = jax.random.split(key)
    shape = (2, COLAT_BLOCKS, LON_BLOCKS, PARTNERS, SLOTS)
    colat_cell = jax.random.randint(key_colat, shape, 0, CT - 1)
    lon_cell = jax.random.randint(key_lon, shape, 0, CP - 1)
    return (lon_cell * CT + colat_cell).astype(jnp.int32)


def draw_ghost_target(key, part):
    key = jax.random.fold_in(key, 14)
    ghost_pos = jnp.arange(GHOSTS)[None, None, None, :]
    colat_block = jnp.arange(COLAT_BLOCKS)[None, :, None, None]
    lon_block = jnp.arange(LON_BLOCKS)[None, None, :, None]
    edge = (ghost_pos < CT) & (lon_block == 0) | (ghost_pos >= CT) & (ghost_pos < 2 * CT) & (lon_block == LON_BLOCKS - 1)
    edge = edge | (ghost_pos >= 2 * CT) & (ghost_pos < 2 * CT + CP) & (colat_block == 0)
    edge = edge | (ghost_pos >= 2 * CT + CP) & (colat_block == COLAT_BLOCKS - 1)
    random_keys = jax.random.randint(key, (2, COLAT_BLOCKS, LON_BLOCKS, GHOSTS), 0, 2 ** 20)
    score = random_keys * GHOSTS + ghost_pos + jnp.where(edge, 0, 2 ** 30)
    order = jnp.argsort(score, axis=-1, stable=True)
    order = jnp.concatenate([order, jnp.full((2, COLAT_BLOCKS, LON_BLOCKS, PARTNERS * SLOTS), GHOSTS, order.dtype)], -1)
    leading = order[..., :PARTNERS * SLOTS]
    edge_count = jnp.sum(edge.astype(jnp.int32), -1)
    slot_no = jnp.arange(PARTNERS * SLOTS)[None, None, None, :]
    target = jnp.where(slot_no < edge_count[..., None], leading, GHOSTS)
    return target.reshape(2, COLAT_BLOCKS, LON_BLOCKS, PARTNERS, SLOTS).astype(jnp.int32)


def draw_interp_weights(key, part):
    key = jax.random.fold_in(key, 15)
    key_first, key_second = jax.random.split(key)
    shape = (2, COLAT_BLOCKS, LON_BLOCKS, PARTNERS, SLOTS)
    frac_colat = jax.random.uniform(key_first, shape, jnp.float32)
    frac_lon = jax.random.uniform(key_second, shape, jnp.float32)
    weight_sets = jnp.stack([(1.0 - frac_lon) * (1.0 - frac_colat), (1.0 - frac_lon) * frac_colat, frac_lon * (1.0 - frac_colat), frac_lon * frac_colat], axis=-2)
    return weight_sets.astype(jnp.float32)


def steps_of(rng, extent, pieces, low, high):
    def one(axis_at, shards_of):
        heights = jax.random.uniform(jax.random.fold_in(jax.random.fold_in(rng, 6), axis_at), (shards_of,), jnp.float32, low / len(pieces), high / len(pieces))
        return jnp.repeat(jnp.exp(heights), extent[axis_at] // shards_of).reshape((-1,) + (1,) * (len(extent) - axis_at - 1))

    factor_of = one(*pieces[0])
    for cut in pieces[1:]:
        factor_of = factor_of * one(*cut)
    return factor_of


def noise(own_key, extent, deviation, reach, pieces=(), held_as=jnp.bfloat16):
    result = deviation * jax.random.normal(own_key, extent, jnp.float32)
    if pieces:
        result = result * steps_of(own_key, extent, pieces, -0.22, 0.18)
    return jnp.clip(result, -reach, reach).astype(held_as)


def setup_inputs(seed: int = 0) -> dict:
    seeds = jax.random.split(jax.random.key(seed), 10)
    state = noise(seeds[0], (2, 4, NR, NP, NT), 1.0, 6.0, ((0, 2), (3, 4), (4, 4)), jnp.float32)
    rhs = noise(seeds[1], (2, 4, NR, NP, NT), 1.0, 6.0, ((0, 2), (3, 4), (4, 4)), jnp.float32)
    viscosity = jnp.clip(jnp.exp(math.log(4.0) - 2.7725887 * jax.random.uniform(seeds[2], (2, NR, NP, NT), jnp.float32) ** steps_of(seeds[2], (2, NR, NP, NT), ((0, 2), (2, 4), (3, 4)), -0.2, 0.2)), 0.25, 4.0)
    radial_bounds = draw_radial_bounds(jax.random.fold_in(seeds[9], 71), 0)
    partner_device = draw_partner_device(jax.random.fold_in(seeds[9], 71), 0)
    ghost_source = draw_ghost_source(jax.random.fold_in(seeds[9], 71), 0)
    ghost_target = draw_ghost_target(jax.random.fold_in(seeds[9], 71), 0)
    interp_weights = draw_interp_weights(jax.random.fold_in(seeds[9], 71), 0)
    rotation = jnp.clip(jax.random.uniform(seeds[8], (2, COLAT_BLOCKS, LON_BLOCKS, PARTNERS, SLOTS), jnp.float32, -3.140625, 3.140625), -3.140625, 3.140625)
    return dict(state=state, rhs=rhs, viscosity=viscosity, radial_bounds=radial_bounds, partner_device=partner_device, ghost_source=ghost_source, ghost_target=ghost_target, interp_weights=interp_weights, rotation=rotation)


OMEGA = 0.6
PRESSURE_STEP = 0.25


def viscous_links(eta_pad):
    centre = eta_pad[1:-1, 1:-1, 1:-1]
    terms = (0.5 * (centre + eta_pad[2:, 1:-1, 1:-1]), 0.5 * (centre + eta_pad[:-2, 1:-1, 1:-1]),
             0.5 * (centre + eta_pad[1:-1, 2:, 1:-1]), 0.5 * (centre + eta_pad[1:-1, :-2, 1:-1]),
             0.5 * (centre + eta_pad[1:-1, 1:-1, 2:]), 0.5 * (centre + eta_pad[1:-1, 1:-1, :-2]))
    diagonal = terms[0] + terms[1] + terms[2] + terms[3] + terms[4] + terms[5]
    return terms, diagonal


def operate(padded, terms):
    centre = padded[:, 1:-1, 1:-1, 1:-1]
    rad_up = padded[:, 2:, 1:-1, 1:-1]
    rad_dn = padded[:, :-2, 1:-1, 1:-1]
    lon_up = padded[:, 1:-1, 2:, 1:-1]
    lon_dn = padded[:, 1:-1, :-2, 1:-1]
    col_up = padded[:, 1:-1, 1:-1, 2:]
    col_dn = padded[:, 1:-1, 1:-1, :-2]
    velocity = centre[:3]
    viscous = terms[0] * (velocity - rad_up[:3]) + terms[1] * (velocity - rad_dn[:3])
    viscous = viscous + terms[2] * (velocity - lon_up[:3]) + terms[3] * (velocity - lon_dn[:3])
    viscous = viscous + terms[4] * (velocity - col_up[:3]) + terms[5] * (velocity - col_dn[:3])
    pressure = centre[3]
    gradient = jnp.stack([pressure - rad_dn[3], pressure - col_dn[3], pressure - lon_dn[3]])
    divergence = (rad_up[0] - centre[0]) + (col_up[1] - centre[1]) + (lon_up[2] - centre[2])
    return jnp.concatenate([viscous + gradient, -divergence[None]], 0)


def blend(corner_vals, weight_rows):
    total = corner_vals[0] * weight_rows[0] + corner_vals[1] * weight_rows[1]
    total = total + corner_vals[2] * weight_rows[2]
    return total + corner_vals[3] * weight_rows[3]


def turn(values, angles):
    cosine = jnp.cos(angles)
    sine_part = jnp.sin(angles)
    colat_part = cosine * values[1] - sine_part * values[2]
    lon_part = sine_part * values[1] + cosine * values[2]
    return jnp.stack([values[0], colat_part, lon_part, values[3]])


def correction(residual, diagonal, visc_cells):
    return jnp.concatenate([OMEGA * residual[:3] / diagonal, -PRESSURE_STEP * visc_cells * residual[3:]], 0)


def ghost_layout(panel_no, partner_device, ghost_source, ghost_target, interp_weights, rotation):
    partner = partner_device[panel_no]
    partner_colat = (partner // LON_BLOCKS)[..., None]
    partner_lon = (partner % LON_BLOCKS)[..., None]
    source = ghost_source[panel_no]
    glob_lon = partner_lon * CP + source // CT
    glob_colat = partner_colat * CT + source % CT
    base = (glob_lon * NT + glob_colat).reshape(-1).astype(jnp.int32)
    weight_rows = jnp.moveaxis(interp_weights[panel_no], -2, 0).reshape(4, -1)
    angles = rotation[panel_no].reshape(-1)
    ghost_pos = ghost_target[panel_no]
    colat_block = jnp.arange(COLAT_BLOCKS).astype(jnp.int32)[:, None, None, None]
    lon_block = jnp.arange(LON_BLOCKS).astype(jnp.int32)[None, :, None, None]
    lo_lon = ghost_pos < CT
    hi_lon = (ghost_pos >= CT) & (ghost_pos < 2 * CT)
    lo_col = (ghost_pos >= 2 * CT) & (ghost_pos < 2 * CT + CP)
    pad_lon = jnp.where(lo_lon, lon_block * CP, jnp.where(hi_lon, (lon_block + 1) * CP + 1,
              jnp.where(lo_col, lon_block * CP + ghost_pos - 2 * CT + 1, lon_block * CP + ghost_pos - 2 * CT - CP + 1)))
    pad_colat = jnp.where(lo_lon, colat_block * CT + ghost_pos + 1, jnp.where(hi_lon, colat_block * CT + ghost_pos - CT + 1,
                jnp.where(lo_col, colat_block * CT, (colat_block + 1) * CT + 1)))
    spots = jnp.where(ghost_pos < GHOSTS, pad_lon * (NT + 2) + pad_colat, (NP + 2) * (NT + 2))
    return base, weight_rows, angles, spots.reshape(-1).astype(jnp.int32)


def padded_panel(masked_self, masked_other, layout):
    base, weight_rows, angles, spots = layout
    features = 4 * NR
    source = masked_other.reshape(features, NP * NT)
    corner_vals = [jnp.take(source, base + offset, axis=1) for offset in (0, 1, NT, NT + 1)]
    values = turn(blend(corner_vals, weight_rows).reshape(4, NR, -1), angles).reshape(features, -1)
    cycle = jnp.zeros((features, (NP + 2) * (NT + 2)), jnp.float32).at[:, spots].add(values, mode="drop")
    padded = cycle.reshape(4, NR, NP + 2, NT + 2).at[:, :, 1:-1, 1:-1].set(masked_self)
    return jnp.pad(padded, ((0, 0), (1, 1), (0, 0), (0, 0)))


def reference(state, rhs, viscosity, radial_bounds, partner_device, ghost_source, ghost_target, interp_weights, rotation):
    levels = jnp.arange(NR).astype(jnp.int32)[None, :]
    active = ((levels >= radial_bounds[:, 0:1]) & (levels < radial_bounds[:, 1:2])).astype(jnp.float32)
    active = active[:, None, :, None, None]
    link_sets = [viscous_links(jnp.pad(viscosity[panel_no], 1)) for panel_no in range(2)]
    layouts = [ghost_layout(panel_no, partner_device, ghost_source, ghost_target, interp_weights, rotation) for panel_no in range(2)]

    def residual_of(current):
        masked = current * active
        results = []
        for panel_no in range(2):
            padded = padded_panel(masked[panel_no], masked[1 - panel_no], layouts[panel_no])
            applied = operate(padded, link_sets[panel_no][0])
            results.append(active[panel_no] * (rhs[panel_no] - applied))
        return jnp.stack(results)

    current = state
    for sweep_no in range(2):
        residual = residual_of(current)
        current = current + jnp.stack([correction(residual[panel_no], link_sets[panel_no][1], viscosity[panel_no]) for panel_no in range(2)])
    residual = residual_of(current)
    return current, residual
```

```python
import jax
import jax.numpy as jnp
from jax import lax
from jax.experimental import pallas as pl
from jax.experimental.pallas import tpu as pltpu
from jax.sharding import PartitionSpec as P

OMEGA = 0.6
PRESSURE_STEP = 0.25
PEERS = 15
F32 = jnp.float32
BF16 = jnp.bfloat16
MESH = pl.DeviceIdType.MESH


def kernel(colats, lons, act_ref, state_ref, rhs_ref, visc_ref, req_ref, cs_ref,
           xo_ref, ro_ref,
           mk, ve, klon, kcu, kcd, kru, krd, dg, dinv, whi, wlo, oh, rx,
           slon, rlon, scol, rcol, vscol, vrcol, vrlon, sg, rg,
           hsend, hrecv, gsend, grecv):
    width = state_ref.shape[1]
    count = colats * lons
    panel = lax.axis_index("panel")
    colat = lax.axis_index("colat")
    lon = lax.axis_index("lon")
    me = colat * lons + lon

    def other(offset):
        number = lax.rem(me + offset + count, count)
        return (1 - panel, lax.div(number, lons), lax.rem(number, lons))

    lon_dn = (panel, colat, lax.rem(lon + lons - 1, lons))
    lon_up = (panel, colat, lax.rem(lon + 1, lons))
    col_dn = (panel, lax.rem(colat + colats - 1, colats), lon)
    col_up = (panel, lax.rem(colat + 1, colats), lon)

    barrier = pltpu.get_barrier_semaphore()
    greeted = [o for o in range(-8, 9)][: min(17, count)]
    for offset in greeted:
        pl.semaphore_signal(barrier, inc=1, device_id=other(offset), device_id_type=MESH)
    for target in (lon_dn, lon_up, col_dn, col_up):
        pl.semaphore_signal(barrier, inc=1, device_id=target, device_id_type=MESH)

    lane = lax.broadcasted_iota(jnp.int32, (8, 128), 1)
    row = lax.broadcasted_iota(jnp.int32, (8, 128), 0)
    first_lane = lane == 0
    last_lane = lane == 127
    top = row == 7
    bottom = row == 0
    act = act_ref[...]
    has_lon_dn = jnp.where(lon > 0, 1.0, 0.0).astype(F32)
    has_lon_up = jnp.where(lon < lons - 1, 1.0, 0.0).astype(F32)
    has_col_dn = jnp.where(colat > 0, 1.0, 0.0).astype(F32)
    has_col_up = jnp.where(colat < colats - 1, 1.0, 0.0).astype(F32)
    zero = jnp.zeros((8, 128), F32)

    def rad_up(x):
        return jnp.where(top, 0.0, pltpu.roll(x, 7, 0))

    def rad_dn(x):
        return jnp.where(bottom, 0.0, pltpu.roll(x, 1, 0))

    def cup(x, halo, i):
        return jnp.where(last_lane, pltpu.roll(halo, 127 - i, 1), pltpu.roll(x, 127, 1))

    def cdn(x, halo, i):
        return jnp.where(first_lane, pltpu.roll(halo, lax.rem(128 - i, 128), 1), pltpu.roll(x, 1, 1))

    def pack(x, i, low, high):
        here = lane == i
        low = jnp.where(here, pltpu.roll(x, i, 1), low)
        high = jnp.where(here, pltpu.roll(x, lax.rem(i + 1, 128), 1), high)
        return low, high

    def send(src, dst, k, target, sends, recvs):
        return pltpu.make_async_remote_copy(
            src_ref=src, dst_ref=dst, send_sem=sends.at[k], recv_sem=recvs.at[k],
            device_id=target, device_id_type=MESH)

    def first(p, carry):
        low, high, vlow, vhigh = carry
        for c in range(4):
            x = state_ref[c, p] * act
            mk[0, c, p + 1] = x
            low, high = pack(x, c * 32 + p, low, high)
        e = visc_ref[p]
        ve[p + 1] = e
        vlow, vhigh = pack(e, p, vlow, vhigh)
        return low, high, vlow, vhigh

    low, high, vlow, vhigh = lax.fori_loop(0, width, first, (zero, zero, zero, zero))
    vscol[0] = vlow
    vscol[1] = vhigh
    rx[15] = zero
    for r in range(3):
        rg[r, 15] = zero

    pl.semaphore_wait(barrier, len(greeted) + 4)

    def request(m):
        return send(req_ref.at[m], rx.at[m], 45 + m, other(m - 8), gsend, grecv)

    def start_request(m, _):
        request(m).start()
        return 0

    lax.fori_loop(0, PEERS, start_request, 0)

    def halo_copies(r):
        return [
            send(slon.at[r, 0], rlon.at[r, 1], 4 * r + 0, lon_dn, hsend, hrecv),
            send(slon.at[r, 1], rlon.at[r, 0], 4 * r + 1, lon_up, hsend, hrecv),
            send(scol.at[r, 0], rcol.at[r, 1], 4 * r + 2, col_dn, hsend, hrecv),
            send(scol.at[r, 1], rcol.at[r, 0], 4 * r + 3, col_up, hsend, hrecv),
        ]

    visc_copies = [
        send(visc_ref.at[0], vrlon.at[1], 12, lon_dn, hsend, hrecv),
        send(visc_ref.at[width - 1], vrlon.at[0], 13, lon_up, hsend, hrecv),
        send(vscol.at[0], vrcol.at[1], 14, col_dn, hsend, hrecv),
        send(vscol.at[1], vrcol.at[0], 15, col_up, hsend, hrecv),
    ]
    for copy in visc_copies:
        copy.start()

    def start_halos(r, low, high):
        for c in range(4):
            slon[r, 0, c] = mk[r % 2, c, 1]
            slon[r, 1, c] = mk[r % 2, c, width]
        scol[r, 0] = low
        scol[r, 1] = high
        for copy in halo_copies(r):
            copy.start()

    start_halos(0, low, high)

    req = req_ref[...].reshape(128, 128)
    column = lax.broadcasted_iota(jnp.int32, (128, 384), 1)
    for j in range(3):
        goal = req[:, 15 + j : 16 + j].astype(jnp.int32) + 320
        oh[j * 128 : (j + 1) * 128, :] = jnp.where(column == goal, 1.0, 0.0).astype(BF16)

    def wait_request(m, _):
        request(m).wait_recv()
        return 0

    lax.fori_loop(0, PEERS, wait_request, 0)
    asked = rx[...].reshape(128, 128)
    wide = lax.broadcasted_iota(jnp.int32, (128, 128), 1)
    for j in range(3):
        src = asked[:, 5 * j : 5 * j + 1].astype(jnp.int32)
        w = [asked[:, 5 * j + 1 + k : 5 * j + 2 + k] for k in range(4)]
        src = jnp.broadcast_to(src, (128, 128))
        src_p = lax.shift_right_logical(src, 7)
        src_t = src - src_p * 128
        near = wide == src_t
        far = wide == src_t + 1
        parts = []
        for a, b in ((w[0], w[1]), (w[2], w[3])):
            u = jnp.where(near, a, jnp.where(far, b, 0.0))
            hi = u.astype(BF16).astype(F32)
            parts.append((hi, u - hi))
        rows = pl.ds(j * 128, 128)

        def build(pp, _, src_p=src_p, parts=parts, rows=rows):
            for h in range(2):
                p = 2 * pp + h
                here = src_p == p
                above = src_p == p - 1
                cols = pl.ds(h * 128, 128)
                whi[pp, rows, cols] = jnp.where(here, parts[0][0], jnp.where(above, parts[1][0], 0.0)).astype(BF16)
                wlo[pp, rows, cols] = jnp.where(here, parts[0][1], jnp.where(above, parts[1][1], 0.0)).astype(BF16)
            return 0

        lax.fori_loop(0, width // 2, build, 0)

    def answer(r, m):
        return send(sg.at[r, m], rg.at[r, m], 15 * r + m, other(8 - m), gsend, grecv)

    nt = (((1,), (1,)), ((), ()))

    def start_answers(r):
        def step(pp, acc):
            x = jnp.concatenate(
                [mk[r % 2, :, 2 * pp + 1].reshape(32, 128), mk[r % 2, :, 2 * pp + 2].reshape(32, 128)], axis=1)
            hi = x.astype(BF16)
            lo = (x - hi.astype(F32)).astype(BF16)
            a = whi[pp]
            acc = acc + lax.dot_general(a, hi, nt, preferred_element_type=F32)
            acc = acc + lax.dot_general(a, lo, nt, preferred_element_type=F32)
            return acc + lax.dot_general(wlo[pp], hi, nt, preferred_element_type=F32)

        v = lax.fori_loop(0, width // 2, step, jnp.zeros((384, 32), F32))
        packed = jnp.concatenate([v[:128], v[128:256], v[256:], jnp.zeros((128, 32), F32)], axis=1)
        sg[r] = packed.reshape(16, 8, 128)

        def go(m, _):
            answer(r, m).start()
            return 0

        lax.fori_loop(0, PEERS, go, 0)

    start_answers(0)

    for copy in visc_copies:
        copy.wait_recv()
    ve[0] = vrlon[0] * has_lon_dn
    ve[width + 1] = vrlon[1] * has_lon_up
    vlow = vrcol[0] * has_col_dn
    vhigh = vrcol[1] * has_col_up
    klon[0] = 0.5 * (ve[0] + ve[1])

    def links(p, _):
        e = ve[p + 1]
        ru = 0.5 * (e + rad_up(e))
        rd = 0.5 * (e + rad_dn(e))
        lu = 0.5 * (e + ve[p + 2])
        ld = 0.5 * (e + ve[p])
        cu = 0.5 * (e + cup(e, vhigh, p))
        cd = 0.5 * (e + cdn(e, vlow, p))
        d = ru + rd + lu + ld + cu + cd
        klon[p + 1] = lu
        kcu[p] = cu
        kcd[p] = cd
        kru[p] = ru
        krd[p] = rd
        dg[p] = d
        dinv[p] = OMEGA / d
        return 0

    lax.fori_loop(0, width, links, 0)

    for r in range(3):
        now, later = r % 2, (r + 1) % 2
        if r > 0:
            start_halos(r, low, high)
            start_answers(r)
        for copy in halo_copies(r):
            copy.wait_recv()

        def wait_answer(m, _, r=r):
            answer(r, m).wait_recv()
            return 0

        lax.fori_loop(0, PEERS, wait_answer, 0)
        turned = jnp.transpose(rg[r].reshape(128, 128))
        vals = jnp.concatenate([turned[0:32], turned[32:64], turned[64:96]], axis=1)
        a = vals.astype(BF16)
        rest = vals - a.astype(F32)
        b = rest.astype(BF16)
        d = (rest - b.astype(F32)).astype(BF16)
        spread = jnp.dot(jnp.concatenate([a, b, d], axis=0), oh[...], preferred_element_type=F32)
        ghost = spread[0:32] + spread[32:64] + spread[64:96]
        cosine = cs_ref[0:1, :]
        sine = cs_ref[1:2, :]
        parts = [ghost[0:8], cosine * ghost[8:16] - sine * ghost[16:24],
                 sine * ghost[8:16] + cosine * ghost[16:24], ghost[24:32]]
        halo_lo = rcol[r, 0] * has_col_dn
        halo_hi = rcol[r, 1] * has_col_up
        for c in range(4):
            mk[now, c, 0] = rlon[r, 0, c] * has_lon_dn + parts[c][:, 0:128]
            mk[now, c, width + 1] = rlon[r, 1, c] * has_lon_up + parts[c][:, 128:256]
            tail = parts[c][:, 256:384]
            inside = (lane >= 32 * c) & (lane < 32 * c + 32)
            lo_part = pltpu.roll(tail, 32 * c, 1) if c else tail
            hi_part = pltpu.roll(tail, (32 * c + 96) % 128, 1) if c != 1 else tail
            halo_lo = halo_lo + jnp.where(inside, lo_part, 0.0)
            halo_hi = halo_hi + jnp.where(inside, hi_part, 0.0)
        source = state_ref if r == 0 else xo_ref

        def sweep(p, carry, r=r, now=now, later=later, halo_lo=halo_lo, halo_hi=halo_hi, source=source):
            low, high = carry
            ru, rd = kru[p], krd[p]
            lu, ld = klon[p + 1], klon[p]
            cu, cd = kcu[p], kcd[p]
            d = dg[p]
            pressure = mk[now, 3, p + 1]
            grad = (pressure - rad_dn(pressure), pressure - cdn(pressure, halo_lo, 96 + p),
                    pressure - mk[now, 3, p])
            div = zero
            res = []
            for c in range(3):
                x = mk[now, c, p + 1]
                i = c * 32 + p
                xru, xlu, xcu = rad_up(x), mk[now, c, p + 2], cup(x, halo_hi, i)
                around = ru * xru + rd * rad_dn(x) + lu * xlu + ld * mk[now, c, p]
                around = around + cu * xcu + cd * cdn(x, halo_lo, i)
                div = div + ((xru, xcu, xlu)[c] - x)
                res.append(act * (rhs_ref[c, p] - ((d * x - around) + grad[c])))
            res.append(act * (rhs_ref[3, p] + div))
            if r == 2:
                for c in range(4):
                    ro_ref[c, p] = res[c]
                return carry
            scale = dinv[p]
            for c in range(4):
                step = scale * res[c] if c < 3 else -PRESSURE_STEP * ve[p + 1] * res[c]
                x = source[c, p] + step
                xo_ref[c, p] = x
                x = x * act
                mk[later, c, p + 1] = x
                low, high = pack(x, c * 32 + p, low, high)
            return low, high

        low, high = lax.fori_loop(0, width, sweep, (zero, zero))

    for copy in visc_copies:
        copy.wait_send()
    for r in range(3):
        for copy in halo_copies(r):
            copy.wait_send()

    def drain(m, _):
        request(m).wait_send()
        for r in range(3):
            answer(r, m).wait_send()
        return 0

    lax.fori_loop(0, PEERS, drain, 0)


def per_device(state, rhs, viscosity, radial_bounds, partner_device, ghost_source,
               ghost_target, interp_weights, rotation):
    components, levels, width_p, width_t = state.shape[1:]
    colats, lons = lax.axis_size("colat"), lax.axis_size("lon")
    count = colats * lons
    me = lax.axis_index("colat") * lons + lax.axis_index("lon")
    level_ids = jnp.arange(levels)
    active = ((level_ids >= radial_bounds[0, 0]) & (level_ids < radial_bounds[0, 1])).astype(F32)
    act = jnp.broadcast_to(active[:, None], (levels, width_t))
    partners = partner_device[0, 0, 0]
    targets = ghost_target[0, 0, 0]
    fields = jnp.concatenate(
        [ghost_source[0, 0, 0].astype(F32)[:, None], interp_weights[0, 0, 0],
         (targets - 320).astype(F32)[:, None]], axis=1)
    fields = jnp.pad(fields, ((0, 0), (0, 0), (0, 4))).reshape(8, 6, 3, 8)
    asks = jnp.transpose(fields[:, :5], (0, 3, 2, 1)).reshape(8, 8, 15)
    goals = jnp.transpose(fields[:, 5], (0, 2, 1))
    rows = jnp.pad(jnp.concatenate([asks, goals], axis=2), ((0, 0), (0, 0), (0, 110)))
    peer = jnp.mod(partners - me + 8 + count, count)
    match = jnp.arange(16)[:, None] == peer[None, :]
    req = jnp.sum(jnp.where(match[:, :, None, None], rows[None], 0.0), axis=1)
    named = targets.reshape(-1)[:, None] == jnp.arange(384)[None, :]
    named = named & (jnp.arange(384)[None, :] < 320)
    angle = jnp.sum(jnp.where(named, rotation[0, 0, 0].reshape(-1)[:, None], 0.0), axis=0)
    cs = jnp.stack([jnp.cos(angle), jnp.sin(angle)])
    block = (components, width_p, levels, width_t)
    vm = pltpu.VMEM
    tile = (levels, width_t)
    row_tiles = (width_p,) + tile
    xo, ro = pl.pallas_call(
        lambda *refs: kernel(colats, lons, *refs),
        out_shape=[jax.ShapeDtypeStruct(block, F32)] * 2,
        in_specs=[pl.BlockSpec(memory_space=pltpu.VMEM)] * 6,
        out_specs=[pl.BlockSpec(memory_space=pltpu.VMEM)] * 2,
        scratch_shapes=[
            vm((2, components, width_p + 2) + tile, F32),
            vm((width_p + 2,) + tile, F32),
            vm((width_p + 1,) + tile, F32),
            vm(row_tiles, F32), vm(row_tiles, F32), vm(row_tiles, F32), vm(row_tiles, F32),
            vm(row_tiles, F32), vm(row_tiles, F32),
            vm((width_p // 2, 384, 256), BF16), vm((width_p // 2, 384, 256), BF16),
            vm((384, 384), BF16),
            vm((16,) + tile, F32),
            vm((3, 2, components) + tile, F32), vm((3, 2, components) + tile, F32),
            vm((3, 2) + tile, F32), vm((3, 2) + tile, F32),
            vm((2,) + tile, F32), vm((2,) + tile, F32), vm((2,) + tile, F32),
            vm((3, 16) + tile, F32), vm((3, 16) + tile, F32),
            pltpu.SemaphoreType.DMA((16,)), pltpu.SemaphoreType.DMA((16,)),
            pltpu.SemaphoreType.DMA((60,)), pltpu.SemaphoreType.DMA((60,)),
        ],
        compiler_params=pltpu.CompilerParams(
            collective_id=0, has_side_effects=True, vmem_limit_bytes=32 * 1024 * 1024),
        name="sweeps",
    )(act, jnp.transpose(state[0], (0, 2, 1, 3)), jnp.transpose(rhs[0], (0, 2, 1, 3)),
      jnp.transpose(viscosity[0], (1, 0, 2)), req, cs)
    back = lambda x: jnp.transpose(x, (0, 2, 1, 3))[None]
    return back(xo), back(ro)


def solution(mesh):
    field = P("panel", None, None, "lon", "colat")
    return jax.shard_map(
        per_device,
        mesh=mesh,
        in_specs=(
            field,
            field,
            P("panel", None, "lon", "colat"),
            P("panel", None),
            P("panel", "colat", "lon", None),
            P("panel", "colat", "lon", None, None),
            P("panel", "colat", "lon", None, None),
            P("panel", "colat", "lon", None, None, None),
            P("panel", "colat", "lon", None, None),
        ),
        out_specs=(field, field),
        check_vma=False,
    )
```

```python
import jax
import jax.numpy as jnp
from jax import lax
from jax.experimental import pallas as pl
from jax.experimental.pallas import tpu as pltpu
from jax.sharding import PartitionSpec as P

OMEGA = 0.6
PRESSURE_STEP = 0.25
PEERS = 15
F32 = jnp.float32
BF16 = jnp.bfloat16
MESH = pl.DeviceIdType.MESH


def blocked(steps, unroll, body, init):
    def block(q, carry):
        for h in range(unroll):
            carry = body(q * unroll + h, carry)
        return carry

    return lax.fori_loop(0, steps // unroll, block, init)


def kernel(colats, lons, bounds_ref, partner_ref, state_ref, rhs_ref, visc_ref, src_ref, tgt_ref, w_ref, rot_ref,
           xo_ref, ro_ref,
           mk, ve, klon, kcu, kcd, kru, krd, dg, dinv, whi, wlo, mhl, oh, fx, req_ref, rx,
           slon, rlon, scol, rcol, vscol, vrcol, vrlon, sg, rg,
           hsend, hrecv, gsend, grecv):
    width = state_ref.shape[1]
    count = colats * lons
    panel = lax.axis_index("panel")
    colat = lax.axis_index("colat")
    lon = lax.axis_index("lon")
    me = colat * lons + lon

    def other(offset):
        number = lax.rem(me + offset + count, count)
        return (1 - panel, lax.div(number, lons), lax.rem(number, lons))

    lon_dn = (panel, colat, lax.rem(lon + lons - 1, lons))
    lon_up = (panel, colat, lax.rem(lon + 1, lons))
    col_dn = (panel, lax.rem(colat + colats - 1, colats), lon)
    col_up = (panel, lax.rem(colat + 1, colats), lon)

    barrier = pltpu.get_barrier_semaphore()
    greeted = [o for o in range(-8, 9)][: min(17, count)]
    for offset in greeted:
        pl.semaphore_signal(barrier, inc=1, device_id=other(offset), device_id_type=MESH)
    for target in (lon_dn, lon_up, col_dn, col_up):
        pl.semaphore_signal(barrier, inc=1, device_id=target, device_id_type=MESH)

    lane = lax.broadcasted_iota(jnp.int32, (8, 128), 1)
    row = lax.broadcasted_iota(jnp.int32, (8, 128), 0)
    first_lane = lane == 0
    last_lane = lane == 127
    top = row == 7
    bottom = row == 0
    act = jnp.where((row >= bounds_ref[0, 0]) & (row < bounds_ref[0, 1]), 1.0, 0.0).astype(F32)
    has_lon_dn = jnp.where(lon > 0, 1.0, 0.0).astype(F32)
    has_lon_up = jnp.where(lon < lons - 1, 1.0, 0.0).astype(F32)
    has_col_dn = jnp.where(colat > 0, 1.0, 0.0).astype(F32)
    has_col_up = jnp.where(colat < colats - 1, 1.0, 0.0).astype(F32)
    zero = jnp.zeros((8, 128), F32)

    def rad_up(x):
        return jnp.where(top, 0.0, pltpu.roll(x, 7, 0))

    def rad_dn(x):
        return jnp.where(bottom, 0.0, pltpu.roll(x, 1, 0))

    def cup(x, halo, i):
        return jnp.where(last_lane, pltpu.roll(halo, 127 - i, 1), pltpu.roll(x, 127, 1))

    def cdn(x, halo, i):
        return jnp.where(first_lane, pltpu.roll(halo, lax.rem(128 - i, 128), 1), pltpu.roll(x, 1, 1))

    def pack(x, i, low, high):
        here = lane == i
        low = jnp.where(here, pltpu.roll(x, i, 1), low)
        high = jnp.where(here, pltpu.roll(x, lax.rem(i + 1, 128), 1), high)
        return low, high

    def send(src, dst, k, target, sends, recvs):
        return pltpu.make_async_remote_copy(
            src_ref=src, dst_ref=dst, send_sem=sends.at[k], recv_sem=recvs.at[k],
            device_id=target, device_id_type=MESH)

    def split(p, xs):
        cols = pl.ds(pl.multiple_of(p * 128, 128), 128)
        for h in range(2):
            x = jnp.concatenate(xs[2 * h : 2 * h + 2], axis=0)
            hi = x.astype(BF16)
            mhl[16 * h : 16 * h + 16, cols] = hi
            mhl[16 * h + 32 : 16 * h + 48, cols] = (x - hi.astype(F32)).astype(BF16)

    slots = src_ref.shape[-1]
    fx[...] = jnp.zeros((128, 128), F32)
    fx[0:8, 0:slots] = src_ref[...].astype(F32)
    for k in range(4):
        fx[8 + 8 * k : 16 + 8 * k, 0:slots] = w_ref[:, k, :]
    fx[40:48, 0:slots] = (tgt_ref[...] - 320).astype(F32)
    fx[48:56, 0:slots] = rot_ref[...]
    by_slot = jnp.transpose(fx[...])
    eighth = lane & 7
    peer = jnp.zeros((8, 128), jnp.int32)
    for k in range(8):
        away = partner_ref[k] - me + 8
        away = jnp.where(away < 0, away + count, away)
        away = jnp.where(away >= count, away - count, away)
        peer = jnp.where(eighth == k, away, peer)
    for m in range(PEERS):
        tile = zero
        for j in range(3):
            t = jnp.where(peer == m, by_slot[8 * j : 8 * j + 8], 0.0)
            for shift in (127, 126, 124):
                t = t + pltpu.roll(t, shift, 1)
            tile = jnp.where(eighth == j, pltpu.roll(t, j, 1) if j else t, tile)
        req_ref[m] = tile
    req_ref[15] = zero
    rx[15] = zero
    for r in range(3):
        rg[r, 15] = zero

    pl.semaphore_wait(barrier, len(greeted) + 4)

    def request(m):
        return send(req_ref.at[m], rx.at[m], 3, other(m - 8), gsend, grecv)

    for m in range(PEERS):
        request(m).start()

    everything = pl.ds(0, PEERS)
    requests = send(req_ref.at[everything], rx.at[everything], 3, other(-8), gsend, grecv)

    def first(p, carry):
        low, high, vlow, vhigh = carry
        xs = [state_ref[c, p] * act for c in range(4)]
        for c, x in enumerate(xs):
            mk[0, c, p + 1] = x
            low, high = pack(x, c * 32 + p, low, high)
        split(p, xs)
        e = visc_ref[p]
        ve[p + 1] = e
        vlow, vhigh = pack(e, p, vlow, vhigh)
        return low, high, vlow, vhigh

    low, high, vlow, vhigh = blocked(width, 8, first, (zero, zero, zero, zero))
    vscol[0] = vlow
    vscol[1] = vhigh

    def halo_copies(r):
        return [
            send(slon.at[r, 0], rlon.at[r, 1], 4 * r + 0, lon_dn, hsend, hrecv),
            send(slon.at[r, 1], rlon.at[r, 0], 4 * r + 1, lon_up, hsend, hrecv),
            send(scol.at[r, 0], rcol.at[r, 1], 4 * r + 2, col_dn, hsend, hrecv),
            send(scol.at[r, 1], rcol.at[r, 0], 4 * r + 3, col_up, hsend, hrecv),
        ]

    visc_copies = [
        send(visc_ref.at[0], vrlon.at[1], 12, lon_dn, hsend, hrecv),
        send(visc_ref.at[width - 1], vrlon.at[0], 13, lon_up, hsend, hrecv),
        send(vscol.at[0], vrcol.at[1], 14, col_dn, hsend, hrecv),
        send(vscol.at[1], vrcol.at[0], 15, col_up, hsend, hrecv),
    ]
    for copy in visc_copies:
        copy.start()

    def start_halos(r, low, high):
        for c in range(4):
            slon[r, 0, c] = mk[r % 2, c, 1]
            slon[r, 1, c] = mk[r % 2, c, width]
        scol[r, 0] = low
        scol[r, 1] = high
        for copy in halo_copies(r):
            copy.start()

    start_halos(0, low, high)

    req = req_ref[...].reshape(128, 128)
    column = lax.broadcasted_iota(jnp.int32, (128, 384), 1)
    angle = jnp.zeros((1, 384), F32)
    for j in range(3):
        goal = req[:, 40 + j : 41 + j].astype(jnp.int32) + 320
        here = column == goal
        oh[j * 128 : (j + 1) * 128, :] = jnp.where(here, 1.0, 0.0).astype(BF16)
        angle = angle + jnp.sum(jnp.where(here, req[:, 48 + j : 49 + j], 0.0), axis=0, keepdims=True)
    cosine = jnp.cos(angle)
    sine = jnp.sin(angle)

    requests.wait_recv()
    asked = rx[...].reshape(128, 128)
    wide = lax.broadcasted_iota(jnp.int32, (128, 128), 1)
    for j in range(3):
        src = asked[:, j : j + 1].astype(jnp.int32)
        w = [asked[:, 8 + 8 * k + j : 9 + 8 * k + j] for k in range(4)]
        src = jnp.broadcast_to(src, (128, 128))
        src_p = lax.shift_right_logical(src, 7)
        src_t = src - src_p * 128
        near = wide == src_t
        far = wide == src_t + 1
        parts = []
        for a, b in ((w[0], w[1]), (w[2], w[3])):
            u = jnp.where(near, a, jnp.where(far, b, 0.0))
            hi = u.astype(BF16).astype(F32)
            parts.append((hi, u - hi))
        rows = pl.ds(j * 128, 128)

        def build(p, _, src_p=src_p, parts=parts, rows=rows):
            here = src_p == p
            above = src_p == p - 1
            cols = pl.ds(pl.multiple_of(p * 128, 128), 128)
            whi[rows, cols] = jnp.where(here, parts[0][0], jnp.where(above, parts[1][0], 0.0)).astype(BF16)
            wlo[rows, cols] = jnp.where(here, parts[0][1], jnp.where(above, parts[1][1], 0.0)).astype(BF16)
            return 0

        blocked(width, 4, build, 0)

    def answer(r, m):
        return send(sg.at[r, m], rg.at[r, m], r, other(8 - m), gsend, grecv)

    def answers(r):
        return send(sg.at[r, everything], rg.at[r, everything], r, other(8), gsend, grecv)

    nt = (((1,), (1,)), ((), ()))

    def start_answers(r):
        v = lax.dot_general(whi[...], mhl[...], nt, preferred_element_type=F32)
        v = v[:, :32] + v[:, 32:] + lax.dot_general(wlo[...], mhl[:32], nt, preferred_element_type=F32)
        packed = jnp.concatenate([v[:128], v[128:256], v[256:], jnp.zeros((128, 32), F32)], axis=1)
        sg[r] = packed.reshape(16, 8, 128)

        for m in range(PEERS):
            answer(r, m).start()

    start_answers(0)

    for copy in visc_copies:
        copy.wait_recv()
    ve[0] = vrlon[0] * has_lon_dn
    ve[width + 1] = vrlon[1] * has_lon_up
    vlow = vrcol[0] * has_col_dn
    vhigh = vrcol[1] * has_col_up
    klon[0] = 0.5 * (ve[0] + ve[1])

    def links(p, _):
        e = ve[p + 1]
        ru = 0.5 * (e + rad_up(e))
        rd = 0.5 * (e + rad_dn(e))
        lu = 0.5 * (e + ve[p + 2])
        ld = 0.5 * (e + ve[p])
        cu = 0.5 * (e + cup(e, vhigh, p))
        cd = 0.5 * (e + cdn(e, vlow, p))
        d = ru + rd + lu + ld + cu + cd
        klon[p + 1] = lu
        kcu[p] = cu
        kcd[p] = cd
        kru[p] = ru
        krd[p] = rd
        dg[p] = d
        dinv[p] = OMEGA / d
        return 0

    blocked(width, 4, links, 0)

    for r in range(3):
        now, later = r % 2, (r + 1) % 2
        if r > 0:
            start_halos(r, low, high)
            start_answers(r)
        for copy in halo_copies(r):
            copy.wait_recv()

        answers(r).wait_recv()
        turned = jnp.transpose(rg[r].reshape(128, 128))
        vals = jnp.concatenate([turned[0:32], turned[32:64], turned[64:96]], axis=1)
        a = vals.astype(BF16)
        rest = vals - a.astype(F32)
        b = rest.astype(BF16)
        d = (rest - b.astype(F32)).astype(BF16)
        spread = jnp.dot(jnp.concatenate([a, b, d], axis=0), oh[...], preferred_element_type=F32)
        ghost = spread[0:32] + spread[32:64] + spread[64:96]
        parts = [ghost[0:8], cosine * ghost[8:16] - sine * ghost[16:24],
                 sine * ghost[8:16] + cosine * ghost[16:24], ghost[24:32]]
        halo_lo = rcol[r, 0] * has_col_dn
        halo_hi = rcol[r, 1] * has_col_up
        for c in range(4):
            mk[now, c, 0] = rlon[r, 0, c] * has_lon_dn + parts[c][:, 0:128]
            mk[now, c, width + 1] = rlon[r, 1, c] * has_lon_up + parts[c][:, 128:256]
            tail = parts[c][:, 256:384]
            inside = (lane >= 32 * c) & (lane < 32 * c + 32)
            lo_part = pltpu.roll(tail, 32 * c, 1) if c else tail
            hi_part = pltpu.roll(tail, (32 * c + 96) % 128, 1) if c != 1 else tail
            halo_lo = halo_lo + jnp.where(inside, lo_part, 0.0)
            halo_hi = halo_hi + jnp.where(inside, hi_part, 0.0)
        source = state_ref if r == 0 else xo_ref

        def sweep(p, carry, r=r, now=now, later=later, halo_lo=halo_lo, halo_hi=halo_hi, source=source):
            low, high = carry
            ru, rd = kru[p], krd[p]
            lu, ld = klon[p + 1], klon[p]
            cu, cd = kcu[p], kcd[p]
            d = dg[p]
            pressure = mk[now, 3, p + 1]
            grad = (pressure - rad_dn(pressure), pressure - cdn(pressure, halo_lo, 96 + p),
                    pressure - mk[now, 3, p])
            div = zero
            res = []
            for c in range(3):
                x = mk[now, c, p + 1]
                i = c * 32 + p
                xru, xlu, xcu = rad_up(x), mk[now, c, p + 2], cup(x, halo_hi, i)
                around = ru * xru + rd * rad_dn(x) + lu * xlu + ld * mk[now, c, p]
                around = around + cu * xcu + cd * cdn(x, halo_lo, i)
                div = div + ((xru, xcu, xlu)[c] - x)
                res.append(act * (rhs_ref[c, p] - ((d * x - around) + grad[c])))
            res.append(act * (rhs_ref[3, p] + div))
            if r == 2:
                for c in range(4):
                    ro_ref[c, p] = res[c]
                return carry
            scale = dinv[p]
            xs = []
            for c in range(4):
                step = scale * res[c] if c < 3 else -PRESSURE_STEP * ve[p + 1] * res[c]
                x = source[c, p] + step
                xo_ref[c, p] = x
                x = x * act
                mk[later, c, p + 1] = x
                xs.append(x)
                low, high = pack(x, c * 32 + p, low, high)
            split(p, xs)
            return low, high

        low, high = blocked(width, 8, sweep, (zero, zero))

    for copy in visc_copies:
        copy.wait_send()
    for r in range(3):
        for copy in halo_copies(r):
            copy.wait_send()

    requests.wait_send()
    for r in range(3):
        answers(r).wait_send()


def per_device(state, rhs, viscosity, radial_bounds, partner_device, ghost_source,
               ghost_target, interp_weights, rotation):
    components, levels, width_p, width_t = state.shape[1:]
    colats, lons = lax.axis_size("colat"), lax.axis_size("lon")
    block = (components, width_p, levels, width_t)
    vm = pltpu.VMEM
    tile = (levels, width_t)
    row_tiles = (width_p,) + tile
    xo, ro = pl.pallas_call(
        lambda *refs: kernel(colats, lons, *refs),
        out_shape=[jax.ShapeDtypeStruct(block, F32)] * 2,
        in_specs=[pl.BlockSpec(memory_space=pltpu.SMEM)] * 2 + [pl.BlockSpec(memory_space=pltpu.VMEM)] * 7,
        out_specs=[pl.BlockSpec(memory_space=pltpu.VMEM)] * 2,
        scratch_shapes=[
            vm((2, components, width_p + 2) + tile, F32),
            vm((width_p + 2,) + tile, F32),
            vm((width_p + 1,) + tile, F32),
            vm(row_tiles, F32), vm(row_tiles, F32), vm(row_tiles, F32), vm(row_tiles, F32),
            vm(row_tiles, F32), vm(row_tiles, F32),
            vm((384, width_p * width_t), BF16), vm((384, width_p * width_t), BF16),
            vm((64, width_p * width_t), BF16),
            vm((384, 384), BF16),
            vm((128, 128), F32),
            vm((16,) + tile, F32), vm((16,) + tile, F32),
            vm((3, 2, components) + tile, F32), vm((3, 2, components) + tile, F32),
            vm((3, 2) + tile, F32), vm((3, 2) + tile, F32),
            vm((2,) + tile, F32), vm((2,) + tile, F32), vm((2,) + tile, F32),
            vm((3, 16) + tile, F32), vm((3, 16) + tile, F32),
            pltpu.SemaphoreType.DMA((16,)), pltpu.SemaphoreType.DMA((16,)),
            pltpu.SemaphoreType.DMA((4,)), pltpu.SemaphoreType.DMA((4,)),
        ],
        compiler_params=pltpu.CompilerParams(
            collective_id=0, has_side_effects=True, vmem_limit_bytes=32 * 1024 * 1024),
        name="sweeps",
    )(radial_bounds, partner_device[0, 0, 0], jnp.transpose(state[0], (0, 2, 1, 3)),
      jnp.transpose(rhs[0], (0, 2, 1, 3)), jnp.transpose(viscosity[0], (1, 0, 2)),
      ghost_source[0, 0, 0], ghost_target[0, 0, 0], interp_weights[0, 0, 0], rotation[0, 0, 0])
    back = lambda x: jnp.transpose(x, (0, 2, 1, 3))[None]
    return back(xo), back(ro)


def solution(mesh):
    field = P("panel", None, None, "lon", "colat")
    return jax.shard_map(
        per_device,
        mesh=mesh,
        in_specs=(
            field,
            field,
            P("panel", None, "lon", "colat"),
            P("panel", None),
            P("panel", "colat", "lon", None),
            P("panel", "colat", "lon", None, None),
            P("panel", "colat", "lon", None, None),
            P("panel", "colat", "lon", None, None, None),
            P("panel", "colat", "lon", None, None),
        ),
        out_specs=(field, field),
        check_vma=False,
    )
```

```python
import jax
import jax.numpy as jnp
from jax import lax
from jax.experimental import pallas as pl
from jax.experimental.pallas import tpu as pltpu
from jax.sharding import PartitionSpec as P

OMEGA = 0.6
PRESSURE_STEP = 0.25
PEERS = 15
F32 = jnp.float32
BF16 = jnp.bfloat16
MESH = pl.DeviceIdType.MESH


def blocked(steps, unroll, body, init):
    def block(q, carry):
        for h in range(unroll):
            carry = body(q * unroll + h, carry)
        return carry

    return lax.fori_loop(0, steps // unroll, block, init)


def kernel(colats, lons, bounds_ref, partner_ref, rhs_in, state_ref, visc_ref, src_ref, tgt_ref, w_ref, rot_ref,
           xo_ref, ro_ref,
           rhs_ref, mk, ve, klon, kcu, kcd, kru, krd, dg, dinv, whi, wlo, mhl, oh, fx, req_ref, rx,
           slon, rlon, scol, rcol, vscol, vrcol, vrlon, sg, rg,
           hsend, hrecv, gsend, grecv, loads):
    width = state_ref.shape[1]
    count = colats * lons
    panel = lax.axis_index("panel")
    colat = lax.axis_index("colat")
    lon = lax.axis_index("lon")
    me = colat * lons + lon

    def other(offset):
        number = lax.rem(me + offset + count, count)
        return (1 - panel, lax.div(number, lons), lax.rem(number, lons))

    lon_dn = (panel, colat, lax.rem(lon + lons - 1, lons))
    lon_up = (panel, colat, lax.rem(lon + 1, lons))
    col_dn = (panel, lax.rem(colat + colats - 1, colats), lon)
    col_up = (panel, lax.rem(colat + 1, colats), lon)

    rhs_loads = []
    for l in range(8):
        rhs_loads.append(pltpu.make_async_copy(rhs_in.at[:, l], rhs_ref.at[:, :, l], loads.at[l]))
    for copy in rhs_loads:
        copy.start()

    barrier = pltpu.get_barrier_semaphore()
    greeted = [o for o in range(-8, 9)][: min(17, count)]
    for offset in greeted:
        pl.semaphore_signal(barrier, inc=1, device_id=other(offset), device_id_type=MESH)
    for target in (lon_dn, lon_up, col_dn, col_up):
        pl.semaphore_signal(barrier, inc=1, device_id=target, device_id_type=MESH)

    lane = lax.broadcasted_iota(jnp.int32, (8, 128), 1)
    row = lax.broadcasted_iota(jnp.int32, (8, 128), 0)
    first_lane = lane == 0
    last_lane = lane == 127
    top = row == 7
    bottom = row == 0
    act = jnp.where((row >= bounds_ref[0, 0]) & (row < bounds_ref[0, 1]), 1.0, 0.0).astype(F32)
    has_lon_dn = jnp.where(lon > 0, 1.0, 0.0).astype(F32)
    has_lon_up = jnp.where(lon < lons - 1, 1.0, 0.0).astype(F32)
    has_col_dn = jnp.where(colat > 0, 1.0, 0.0).astype(F32)
    has_col_up = jnp.where(colat < colats - 1, 1.0, 0.0).astype(F32)
    zero = jnp.zeros((8, 128), F32)

    def rad_up(x):
        return jnp.where(top, 0.0, pltpu.roll(x, 7, 0))

    def rad_dn(x):
        return jnp.where(bottom, 0.0, pltpu.roll(x, 1, 0))

    def cup(x, halo, i):
        return jnp.where(last_lane, pltpu.roll(halo, 127 - i, 1), pltpu.roll(x, 127, 1))

    def cdn(x, halo, i):
        return jnp.where(first_lane, pltpu.roll(halo, lax.rem(128 - i, 128), 1), pltpu.roll(x, 1, 1))

    def pack(x, i, low, high):
        here = lane == i
        low = jnp.where(here, pltpu.roll(x, i, 1), low)
        high = jnp.where(here, pltpu.roll(x, lax.rem(i + 1, 128), 1), high)
        return low, high

    def send(src, dst, k, target, sends, recvs):
        return pltpu.make_async_remote_copy(
            src_ref=src, dst_ref=dst, send_sem=sends.at[k], recv_sem=recvs.at[k],
            device_id=target, device_id_type=MESH)

    def split(p, xs):
        cols = pl.ds(pl.multiple_of(p * 128, 128), 128)
        for h in range(2):
            x = jnp.concatenate(xs[2 * h : 2 * h + 2], axis=0)
            hi = x.astype(BF16)
            mhl[16 * h : 16 * h + 16, cols] = hi
            mhl[16 * h + 32 : 16 * h + 48, cols] = (x - hi.astype(F32)).astype(BF16)

    slots = src_ref.shape[-1]
    fx[...] = jnp.zeros((128, 128), F32)
    fx[0:8, 0:slots] = src_ref[...].astype(F32)
    for k in range(4):
        fx[8 + 8 * k : 16 + 8 * k, 0:slots] = w_ref[:, k, :]
    fx[40:48, 0:slots] = (tgt_ref[...] - 320).astype(F32)
    fx[48:56, 0:slots] = rot_ref[...]
    by_slot = jnp.transpose(fx[...])
    eighth = lane & 7
    peer = jnp.zeros((8, 128), jnp.int32)
    for k in range(8):
        away = partner_ref[k] - me + 8
        away = jnp.where(away < 0, away + count, away)
        away = jnp.where(away >= count, away - count, away)
        peer = jnp.where(eighth == k, away, peer)
    for m in range(PEERS):
        tile = zero
        for j in range(3):
            t = jnp.where(peer == m, by_slot[8 * j : 8 * j + 8], 0.0)
            for shift in (127, 126, 124):
                t = t + pltpu.roll(t, shift, 1)
            tile = jnp.where(eighth == j, pltpu.roll(t, j, 1) if j else t, tile)
        req_ref[m] = tile
    req_ref[15] = zero
    rx[15] = zero
    for r in range(3):
        rg[r, 15] = zero

    pl.semaphore_wait(barrier, len(greeted) + 4)

    def request(m):
        return send(req_ref.at[m], rx.at[m], 3, other(m - 8), gsend, grecv)

    for m in range(PEERS):
        request(m).start()

    everything = pl.ds(0, PEERS)
    requests = send(req_ref.at[everything], rx.at[everything], 3, other(-8), gsend, grecv)

    def first(p, carry):
        low, high, vlow, vhigh = carry
        xs = [state_ref[c, p] * act for c in range(4)]
        for c, x in enumerate(xs):
            mk[0, c, p + 1] = x
            low, high = pack(x, c * 32 + p, low, high)
        split(p, xs)
        e = visc_ref[p]
        ve[p + 1] = e
        vlow, vhigh = pack(e, p, vlow, vhigh)
        return low, high, vlow, vhigh

    low, high, vlow, vhigh = blocked(width, 8, first, (zero, zero, zero, zero))
    vscol[0] = vlow
    vscol[1] = vhigh

    def halo_copies(r):
        return [
            send(slon.at[r, 0], rlon.at[r, 1], 4 * r + 0, lon_dn, hsend, hrecv),
            send(slon.at[r, 1], rlon.at[r, 0], 4 * r + 1, lon_up, hsend, hrecv),
            send(scol.at[r, 0], rcol.at[r, 1], 4 * r + 2, col_dn, hsend, hrecv),
            send(scol.at[r, 1], rcol.at[r, 0], 4 * r + 3, col_up, hsend, hrecv),
        ]

    visc_copies = [
        send(visc_ref.at[0], vrlon.at[1], 12, lon_dn, hsend, hrecv),
        send(visc_ref.at[width - 1], vrlon.at[0], 13, lon_up, hsend, hrecv),
        send(vscol.at[0], vrcol.at[1], 14, col_dn, hsend, hrecv),
        send(vscol.at[1], vrcol.at[0], 15, col_up, hsend, hrecv),
    ]
    for copy in visc_copies:
        copy.start()

    def start_halos(r, low, high):
        for c in range(4):
            slon[r, 0, c] = mk[r % 2, c, 1]
            slon[r, 1, c] = mk[r % 2, c, width]
        scol[r, 0] = low
        scol[r, 1] = high
        for copy in halo_copies(r):
            copy.start()

    start_halos(0, low, high)

    req = req_ref[...].reshape(128, 128)
    column = lax.broadcasted_iota(jnp.int32, (128, 384), 1)
    angle = jnp.zeros((1, 384), F32)
    for j in range(3):
        goal = req[:, 40 + j : 41 + j].astype(jnp.int32) + 320
        here = column == goal
        oh[j * 128 : (j + 1) * 128, :] = jnp.where(here, 1.0, 0.0).astype(BF16)
        angle = angle + jnp.sum(jnp.where(here, req[:, 48 + j : 49 + j], 0.0), axis=0, keepdims=True)
    cosine = jnp.cos(angle)
    sine = jnp.sin(angle)

    requests.wait_recv()
    asked = rx[...].reshape(128, 128)
    wide = lax.broadcasted_iota(jnp.int32, (128, 128), 1)
    for j in range(3):
        src = asked[:, j : j + 1].astype(jnp.int32)
        w = [asked[:, 8 + 8 * k + j : 9 + 8 * k + j] for k in range(4)]
        src = jnp.broadcast_to(src, (128, 128))
        src_p = lax.shift_right_logical(src, 7)
        src_t = src - src_p * 128
        near = wide == src_t
        far = wide == src_t + 1
        parts = []
        for a, b in ((w[0], w[1]), (w[2], w[3])):
            u = jnp.where(near, a, jnp.where(far, b, 0.0))
            hi = u.astype(BF16).astype(F32)
            parts.append((hi, u - hi))
        rows = pl.ds(j * 128, 128)

        def build(p, _, src_p=src_p, parts=parts, rows=rows):
            here = src_p == p
            above = src_p == p - 1
            cols = pl.ds(pl.multiple_of(p * 128, 128), 128)
            whi[rows, cols] = jnp.where(here, parts[0][0], jnp.where(above, parts[1][0], 0.0)).astype(BF16)
            wlo[rows, cols] = jnp.where(here, parts[0][1], jnp.where(above, parts[1][1], 0.0)).astype(BF16)
            return 0

        blocked(width, 4, build, 0)

    def answer(r, m):
        return send(sg.at[r, m], rg.at[r, m], r, other(8 - m), gsend, grecv)

    def answers(r):
        return send(sg.at[r, everything], rg.at[r, everything], r, other(8), gsend, grecv)

    nt = (((1,), (1,)), ((), ()))

    def start_answers(r):
        v = lax.dot_general(whi[...], mhl[...], nt, preferred_element_type=F32)
        v = v[:, :32] + v[:, 32:] + lax.dot_general(wlo[...], mhl[:32], nt, preferred_element_type=F32)
        packed = jnp.concatenate([v[:128], v[128:256], v[256:], jnp.zeros((128, 32), F32)], axis=1)
        sg[r] = packed.reshape(16, 8, 128)

        for m in range(PEERS):
            answer(r, m).start()

    start_answers(0)

    for copy in visc_copies:
        copy.wait_recv()
    ve[0] = vrlon[0] * has_lon_dn
    ve[width + 1] = vrlon[1] * has_lon_up
    vlow = vrcol[0] * has_col_dn
    vhigh = vrcol[1] * has_col_up
    klon[0] = 0.5 * (ve[0] + ve[1])

    def links(p, _):
        e = ve[p + 1]
        ru = 0.5 * (e + rad_up(e))
        rd = 0.5 * (e + rad_dn(e))
        lu = 0.5 * (e + ve[p + 2])
        ld = 0.5 * (e + ve[p])
        cu = 0.5 * (e + cup(e, vhigh, p))
        cd = 0.5 * (e + cdn(e, vlow, p))
        d = ru + rd + lu + ld + cu + cd
        klon[p + 1] = lu
        kcu[p] = cu
        kcd[p] = cd
        kru[p] = ru
        krd[p] = rd
        dg[p] = d
        dinv[p] = OMEGA / d
        return 0

    blocked(width, 4, links, 0)

    for copy in rhs_loads:
        copy.wait()
    for r in range(3):
        now, later = r % 2, (r + 1) % 2
        if r > 0:
            start_halos(r, low, high)
            start_answers(r)
        for copy in halo_copies(r):
            copy.wait_recv()

        answers(r).wait_recv()
        turned = jnp.transpose(rg[r].reshape(128, 128))
        vals = jnp.concatenate([turned[0:32], turned[32:64], turned[64:96]], axis=1)
        a = vals.astype(BF16)
        rest = vals - a.astype(F32)
        b = rest.astype(BF16)
        d = (rest - b.astype(F32)).astype(BF16)
        spread = jnp.dot(jnp.concatenate([a, b, d], axis=0), oh[...], preferred_element_type=F32)
        ghost = spread[0:32] + spread[32:64] + spread[64:96]
        parts = [ghost[0:8], cosine * ghost[8:16] - sine * ghost[16:24],
                 sine * ghost[8:16] + cosine * ghost[16:24], ghost[24:32]]
        halo_lo = rcol[r, 0] * has_col_dn
        halo_hi = rcol[r, 1] * has_col_up
        for c in range(4):
            mk[now, c, 0] = rlon[r, 0, c] * has_lon_dn + parts[c][:, 0:128]
            mk[now, c, width + 1] = rlon[r, 1, c] * has_lon_up + parts[c][:, 128:256]
            tail = parts[c][:, 256:384]
            inside = (lane >= 32 * c) & (lane < 32 * c + 32)
            lo_part = pltpu.roll(tail, 32 * c, 1) if c else tail
            hi_part = pltpu.roll(tail, (32 * c + 96) % 128, 1) if c != 1 else tail
            halo_lo = halo_lo + jnp.where(inside, lo_part, 0.0)
            halo_hi = halo_hi + jnp.where(inside, hi_part, 0.0)
        source = state_ref if r == 0 else xo_ref

        def sweep(p, carry, r=r, now=now, later=later, halo_lo=halo_lo, halo_hi=halo_hi, source=source):
            low, high = carry
            ru, rd = kru[p], krd[p]
            lu, ld = klon[p + 1], klon[p]
            cu, cd = kcu[p], kcd[p]
            d = dg[p]
            pressure = mk[now, 3, p + 1]
            grad = (pressure - rad_dn(pressure), pressure - cdn(pressure, halo_lo, 96 + p),
                    pressure - mk[now, 3, p])
            div = zero
            res = []
            for c in range(3):
                x = mk[now, c, p + 1]
                i = c * 32 + p
                xru, xlu, xcu = rad_up(x), mk[now, c, p + 2], cup(x, halo_hi, i)
                around = ru * xru + rd * rad_dn(x) + lu * xlu + ld * mk[now, c, p]
                around = around + cu * xcu + cd * cdn(x, halo_lo, i)
                div = div + ((xru, xcu, xlu)[c] - x)
                res.append(act * (rhs_ref[c, p] - ((d * x - around) + grad[c])))
            res.append(act * (rhs_ref[3, p] + div))
            if r == 2:
                for c in range(4):
                    ro_ref[c, p] = res[c]
                return carry
            scale = dinv[p]
            xs = []
            for c in range(4):
                step = scale * res[c] if c < 3 else -PRESSURE_STEP * ve[p + 1] * res[c]
                x = source[c, p] + step
                xo_ref[c, p] = x
                x = x * act
                mk[later, c, p + 1] = x
                xs.append(x)
                low, high = pack(x, c * 32 + p, low, high)
            split(p, xs)
            return low, high

        low, high = blocked(width, 8, sweep, (zero, zero))

    for copy in visc_copies:
        copy.wait_send()
    for r in range(3):
        for copy in halo_copies(r):
            copy.wait_send()

    requests.wait_send()
    for r in range(3):
        answers(r).wait_send()


def per_device(state, rhs, viscosity, radial_bounds, partner_device, ghost_source,
               ghost_target, interp_weights, rotation):
    components, levels, width_p, width_t = state.shape[1:]
    colats, lons = lax.axis_size("colat"), lax.axis_size("lon")
    block = (components, width_p, levels, width_t)
    vm = pltpu.VMEM
    tile = (levels, width_t)
    row_tiles = (width_p,) + tile
    xo, ro = pl.pallas_call(
        lambda *refs: kernel(colats, lons, *refs),
        out_shape=[jax.ShapeDtypeStruct(block, F32)] * 2,
        in_specs=[pl.BlockSpec(memory_space=pltpu.SMEM)] * 2 + [pl.BlockSpec(memory_space=pl.ANY)] + [pl.BlockSpec(memory_space=pltpu.VMEM)] * 6,
        out_specs=[pl.BlockSpec(memory_space=pltpu.VMEM)] * 2,
        scratch_shapes=[
            vm(block, F32),
            vm((2, components, width_p + 2) + tile, F32),
            vm((width_p + 2,) + tile, F32),
            vm((width_p + 1,) + tile, F32),
            vm(row_tiles, F32), vm(row_tiles, F32), vm(row_tiles, F32), vm(row_tiles, F32),
            vm(row_tiles, F32), vm(row_tiles, F32),
            vm((384, width_p * width_t), BF16), vm((384, width_p * width_t), BF16),
            vm((64, width_p * width_t), BF16),
            vm((384, 384), BF16),
            vm((128, 128), F32),
            vm((16,) + tile, F32), vm((16,) + tile, F32),
            vm((3, 2, components) + tile, F32), vm((3, 2, components) + tile, F32),
            vm((3, 2) + tile, F32), vm((3, 2) + tile, F32),
            vm((2,) + tile, F32), vm((2,) + tile, F32), vm((2,) + tile, F32),
            vm((3, 16) + tile, F32), vm((3, 16) + tile, F32),
            pltpu.SemaphoreType.DMA((16,)), pltpu.SemaphoreType.DMA((16,)),
            pltpu.SemaphoreType.DMA((4,)), pltpu.SemaphoreType.DMA((4,)),
            pltpu.SemaphoreType.DMA((8,)),
        ],
        compiler_params=pltpu.CompilerParams(
            collective_id=0, has_side_effects=True, vmem_limit_bytes=32 * 1024 * 1024),
        name="sweeps",
    )(radial_bounds, partner_device[0, 0, 0], rhs[0],
      jnp.transpose(state[0], (0, 2, 1, 3)), jnp.transpose(viscosity[0], (1, 0, 2)),
      ghost_source[0, 0, 0], ghost_target[0, 0, 0], interp_weights[0, 0, 0], rotation[0, 0, 0])
    back = lambda x: jnp.transpose(x, (0, 2, 1, 3))[None]
    return back(xo), back(ro)


def solution(mesh):
    field = P("panel", None, None, "lon", "colat")
    return jax.shard_map(
        per_device,
        mesh=mesh,
        in_specs=(
            field,
            field,
            P("panel", None, "lon", "colat"),
            P("panel", None),
            P("panel", "colat", "lon", None),
            P("panel", "colat", "lon", None, None),
            P("panel", "colat", "lon", None, None),
            P("panel", "colat", "lon", None, None, None),
            P("panel", "colat", "lon", None, None),
        ),
        out_specs=(field, field),
        check_vma=False,
    )
```
